512 devices in a mesh: ctx: 64 (over y_hi, z, core), tp: 8 (over y_lo, x).
Axes of the slice: x: 4, y: 4 (y_hi: 2, y_lo: 2; y = y_hi * 2 + y_lo), z: 16, core: 2. Of those that a mesh axis runs over, the one named last changes fastest.
Arguments:
- queries: bfloat16 [6144, 8192], P(('ctx', 'tp')), may hold values from -200 to 200
- keys: bfloat16 [6144, 1024], P(('ctx', 'tp')), may hold values from -9 to 9
- values: bfloat16 [6144, 1024], P(('ctx', 'tp')), may hold values from -6 to 6
- parent_block: int32 [128], replicated, may hold values from 0 to 126, as said below
- slot_block: int32 [128], replicated, may hold values from 0 to 127, each once
Outputs:
- attended: bfloat16 [6144, 8192], P(('ctx', 'tp'))
The draws below stay inside these ranges and needn't reach their ends.
Inputs may be any that keep to these rules, and one draw needn't show every extreme that they name: parent_block[0] = 0 (block 0 is the root). Blocks 1 to 63 each have the block before as parent (the shared prompt). Then 16 beams of 4 blocks follow: inside a beam each block's parent is the block before; a beam's first block has as parent some earlier block of index 32 or more. slot_block is a permutation; slot j holds rows j * 48 to (j + 1) * 48 - 1.
All inputs are finite; a program needn't handle non-finite values.
Results may differ from the reference program's by a relative error of at most 0.007.
Values may be sent and summed in bfloat16 or wider, within the bound.
No kernel may reach another device: no remote copies, remote signals or barrier semaphores. Data moves between devices by JAX's collectives and lax.ppermute only.
A program may use at most 64 MiB of HBM per device.

```python
import math
import jax
import jax.numpy as jnp
from jax import lax

QUERY_HEADS = 64
KEY_VALUE_HEADS = 8
HEAD_SIZE = 128
BLK = 48
NB = 128
PACKED_TOKENS = 6144
PROMPT_BLOCKS = 64
BEAM_BLOCKS = 4


def shared_keys(key):
    base_random_key = jax.random.truncated_normal(key, -6.0, 6.0, (PACKED_TOKENS, KEY_VALUE_HEADS * HEAD_SIZE), jnp.float32)
    return base_random_key


def draw_keys(key, part):
    key_random_seed = shared_keys(key)
    return key_random_seed.astype(jnp.bfloat16)


def draw_queries(key, part):
    key = jax.random.fold_in(key, 7)
    base_random_key = jax.random.truncated_normal(key, -6.0, 6.0, (PACKED_TOKENS, QUERY_HEADS * HEAD_SIZE), jnp.float32)
    return base_random_key.astype(jnp.bfloat16)


def draw_parent_block(key, part):
    key = jax.random.fold_in(key, 5)
    indices = jnp.arange(NB, dtype=jnp.int32)
    random_picks = jax.random.randint(key, (NB,), 0, 1048576, dtype=jnp.int32)
    half_prompt = PROMPT_BLOCKS // 2
    span_below = jnp.maximum(indices - half_prompt, 1)
    forked = half_prompt + random_picks % span_below
    beam_start = (indices >= PROMPT_BLOCKS) & ((indices - PROMPT_BLOCKS) % BEAM_BLOCKS == 0) & (indices != NB - BEAM_BLOCKS)
    chained = jnp.maximum(indices - 1, 0)
    return jnp.where(beam_start, forked, chained).astype(jnp.int32)


def steps_of(rng, dims, cuts, low, largest):
    factor_of = 1.0
    for dim, blocks in cuts:
        heights = jax.random.uniform(jax.random.fold_in(jax.random.fold_in(rng, 6), dim), (blocks,), jnp.float32, low / len(cuts), largest / len(cuts))
        factor_of = factor_of * jnp.repeat(jnp.exp(heights), dims[dim] // blocks).reshape((-1,) + (1,) * (len(dims) - 1 - dim))
    return factor_of


def noise(rng, extent, scale, reach, cuts=(), kind=jnp.bfloat16):
    drawn = jax.random.normal(rng, extent, jnp.float32) * scale
    if len(cuts) > 0:
        drawn = steps_of(rng, extent, cuts, -0.22, 0.18) * drawn
    return jnp.clip(drawn, min=-reach, max=reach).astype(kind)


def setup_inputs(seed: int = 0) -> dict:
    splits = jax.random.split(jax.random.key(seed), 6)
    return {
        "queries": draw_queries(jax.random.fold_in(splits[5], 71), 0),
        "keys": draw_keys(jax.random.fold_in(splits[5], 71), 0),
        "values": noise(splits[2], (PACKED_TOKENS, KEY_VALUE_HEADS * HEAD_SIZE), 1.0, 6.0, ((0, 512),)),
        "parent_block": draw_parent_block(jax.random.fold_in(splits[5], 71), 0),
        "slot_block": jax.random.permutation(splits[4], NB).astype(jnp.int32),
    }


def ancestors(parent_block, block_count):
    indices = jnp.arange(block_count, dtype=jnp.int32)
    single_step = (parent_block[:, None] == indices[None, :]).astype(jnp.float32)
    identity_table = (indices[:, None] == indices[None, :]).astype(jnp.float32)
    reach_table = jnp.maximum(single_step, identity_table)
    for doubling in range(block_count.bit_length()):
        reach_table = jnp.minimum(jnp.dot(reach_table, reach_table, precision=lax.Precision.HIGHEST, preferred_element_type=jnp.float32), 1.0)
    return reach_table

def reference(queries, keys, values, parent_block, slot_block):
    reach_table = ancestors(parent_block, NB)
    query_group_size = QUERY_HEADS // KEY_VALUE_HEADS
    scale_factor = 1.0 / math.sqrt(HEAD_SIZE)
    positions = jnp.arange(PACKED_TOKENS, dtype=jnp.int32)
    token_block = slot_block[positions // BLK]
    token_offset = positions % BLK
    query_row_tensor = queries.reshape(PACKED_TOKENS, KEY_VALUE_HEADS, query_group_size, HEAD_SIZE)
    key_head_tensor = keys.reshape(PACKED_TOKENS, KEY_VALUE_HEADS, HEAD_SIZE)
    value_head_tensor = values.reshape(PACKED_TOKENS, KEY_VALUE_HEADS, HEAD_SIZE)
    rows_per_block = math.gcd(PACKED_TOKENS, 256)
    total_blocks = PACKED_TOKENS // rows_per_block
    key_rows = math.gcd(PACKED_TOKENS, 256)
    key_total = PACKED_TOKENS // key_rows

    def attend_layer(flattened_index):
        current_row_block = flattened_index // KEY_VALUE_HEADS
        current_head_index = flattened_index % KEY_VALUE_HEADS
        first_row = (current_row_block * rows_per_block).astype(jnp.int32)
        query_part = lax.dynamic_slice_in_dim(query_row_tensor, first_row, rows_per_block, 0)
        query_part = lax.dynamic_index_in_dim(query_part, current_head_index, 1, keepdims=False).astype(jnp.float32)
        key_part = lax.dynamic_index_in_dim(key_head_tensor, current_head_index, 1, keepdims=False)
        value_part = lax.dynamic_index_in_dim(value_head_tensor, current_head_index, 1, keepdims=False)
        query_block = lax.dynamic_slice_in_dim(token_block, first_row, rows_per_block)
        query_offset = lax.dynamic_slice_in_dim(token_offset, first_row, rows_per_block)
        query_reach = reach_table[query_block]

        def piece(key_index):
            first_key = (key_index * key_rows).astype(jnp.int32)
            key_block = lax.dynamic_slice_in_dim(token_block, first_key, key_rows)
            key_offset = lax.dynamic_slice_in_dim(token_offset, first_key, key_rows)
            block_ok = query_reach[:, key_block] > 0.5
            allowed = block_ok & ((query_block[:, None] != key_block[None, :]) | (key_offset[None, :] <= query_offset[:, None]))
            key_slice = lax.dynamic_slice_in_dim(key_part, first_key, key_rows, 0).astype(jnp.float32)
            value_slice = lax.dynamic_slice_in_dim(value_part, first_key, key_rows, 0).astype(jnp.float32)
            return (allowed, key_slice, value_slice)

        def masked_scores(allowed, key_slice):
            scores = jnp.einsum('rgd,nd->rgn', query_part, key_slice) * scale_factor
            return jnp.where(allowed[:, None, :], scores, -1e+30)

        def find_max(highest, key_index):
            allowed, key_slice, value_slice = piece(key_index)
            local_high = lax.cond(jnp.any(allowed), lambda: lax.optimization_barrier(jnp.max(masked_scores(allowed, key_slice), axis=-1)), lambda: jnp.full(highest.shape, -1e+30, highest.dtype))
            return (jnp.maximum(highest, local_high), None)
        highest, unused = lax.scan(find_max, jnp.full((rows_per_block, query_group_size), -1e+30, jnp.float32), jnp.arange(key_total, dtype=jnp.int32))

        def accumulate(running, key_index):
            totals, summed = running
            allowed, key_slice, value_slice = piece(key_index)

            def compute():
                scores = masked_scores(allowed, key_slice)
                exponent = jnp.where(allowed[:, None, :], jnp.exp(scores - highest[..., None]), 0.0)
                weights = lax.optimization_barrier(exponent.astype(jnp.bfloat16)).astype(jnp.float32)
                return (totals + lax.optimization_barrier(jnp.sum(exponent, axis=-1)), summed + jnp.einsum('rgn,nd->rgd', weights, value_slice))
            return (lax.cond(jnp.any(allowed), compute, lambda: (totals, summed)), None)
        start = (jnp.zeros((rows_per_block, query_group_size), jnp.float32), jnp.zeros((rows_per_block, query_group_size, HEAD_SIZE), jnp.float32))
        (totals, summed), unused = lax.scan(accumulate, start, jnp.arange(key_total, dtype=jnp.int32))
        return (summed / totals[..., None]).astype(jnp.bfloat16)
    head_results = lax.map(attend_layer, jnp.arange(total_blocks * KEY_VALUE_HEADS, dtype=jnp.int32))
    head_results = head_results.reshape(total_blocks, KEY_VALUE_HEADS, rows_per_block, query_group_size, HEAD_SIZE).transpose(0, 2, 1, 3, 4)
    return head_results.reshape(PACKED_TOKENS, QUERY_HEADS * HEAD_SIZE)
```

```python
import math

import jax
import jax.numpy as jnp
from jax import lax
from jax.experimental import pallas as pl
from jax.experimental.pallas import tpu as pltpu
from jax.sharding import Mesh
from jax.sharding import PartitionSpec as P

GROUP = 8
HEAD = 128
BLK = 48
NB = 128
Z = 16
SLOTS = 64
CHUNK = 8 * BLK
ROWS = BLK * GROUP
PART = ROWS // 4
SCALE2 = math.log2(math.e) / math.sqrt(HEAD)
LOW = -1e30


def nn(a, b):
    return lax.dot_general(a, b, (((1,), (0,)), ((), ())), preferred_element_type=jnp.float32)


def nt(a, b):
    return lax.dot_general(a, b, (((1,), (1,)), ((), ())), preferred_element_type=jnp.float32)


def table_kernel(parent, slot, table):
    yh, z, c = lax.axis_index("yh"), lax.axis_index("z"), lax.axis_index("c")
    square = (NB, NB)
    row = lax.broadcasted_iota(jnp.int32, square, 0)
    column = lax.broadcasted_iota(jnp.int32, square, 1)
    one = lambda hit: jnp.where(hit, 1.0, 0.0).astype(jnp.bfloat16)
    reach_t = one((parent[...] == row) | (row == column))
    for _ in range(NB.bit_length() - 1):
        reach_t = one(nn(reach_t, reach_t) > 0.5)
    place = one(slot[...] == row)
    s = lax.broadcasted_iota(jnp.int32, (16, NB), 0)
    j = lax.broadcasted_iota(jnp.int32, (16, NB), 1)
    mine = (((s // 2) * Z + z) * 2 + c) * 2 + s % 2
    block = nt(one(j == mine), place).astype(jnp.bfloat16)
    reached = nt(block, reach_t).astype(jnp.bfloat16)
    by_slot = nn(reached, place).astype(jnp.bfloat16)
    core = jnp.where(column < SLOTS // 2, c, 1 - c)
    theirs = ((yh * Z + (column % (SLOTS // 2)) // 2) * 2 + core) * 2 + column % 2
    order = one((row == theirs) & (column < SLOTS))
    own = (s // 2 == yh) & (j == z * 2 + s % 2)
    taken = (nn(by_slot, order) > 0.5) & ~own
    before = nn(one(taken), one(row < column))
    at = jnp.where(taken, before, -1.0)
    number = j.astype(jnp.float32).astype(jnp.bfloat16)
    lists = jnp.zeros((16, NB), jnp.float32)
    for q in range(4):
        hit = one(at[q : q + 1, :] == row.astype(jnp.float32))
        lists = jnp.where(s == q, nt(number, hit), lists)
    counts = jnp.sum(jnp.where(taken, 1.0, 0.0), axis=1, keepdims=True)
    last = (s // 2 == yh) & (j.astype(jnp.float32) == counts)
    lists = jnp.where(last, (z * 2 + s % 2).astype(jnp.float32), lists)
    lists = lists[:4].astype(jnp.int32)
    table[...] = jnp.concatenate([lists, jnp.broadcast_to(counts[:4], (4, NB)).astype(jnp.int32)], axis=0)


def unpack_kernel(received, pairs, spread):
    yh = lax.axis_index("yh")
    tokens = PART // GROUP
    for g in range(8):
        both = received[yh, g, PART : PART + 2 * tokens, :].astype(jnp.float32)
        spread[g * tokens : (g + 1) * tokens, :HEAD] = both[:tokens]
        spread[g * tokens : (g + 1) * tokens, HEAD:] = both[tokens:]
    pairs[...] = spread[...].astype(jnp.bfloat16)


def attend_kernel(table, received, near, far, out, pairs, query, scores, highest, totals, summed):
    yh = lax.axis_index("yh")
    half = SLOTS // 2 * BLK
    pairs[:half, :] = near[...]
    pairs[half:, :] = far[...]
    eye = lax.broadcasted_iota(jnp.int32, (PART, HEAD), 0) == lax.broadcasted_iota(
        jnp.int32, (PART, HEAD), 1
    )
    stat_row = lax.broadcasted_iota(jnp.int32, (16, HEAD), 0)
    tall = (ROWS, HEAD)
    tiles = CHUNK // HEAD
    least = lax.broadcasted_iota(jnp.int32, (1, CHUNK), 1)
    offset = lax.broadcasted_iota(jnp.int32, (ROWS, 1), 0) // GROUP

    def gathered(s, i, columns):
        return jnp.concatenate(
            [
                pairs[pl.ds(pl.multiple_of(table[s, i * 8 + t] * BLK, 16), BLK), columns]
                for t in range(8)
            ],
            axis=0,
        )

    @pl.loop(0, 4)
    def _(s):
        own = jnp.where(s // 2 == yh, 1, 0)
        count = table[4 + s, 0]
        last = jnp.maximum(count + own - 1, 0) // 8
        for x in range(4):
            query[x * PART : (x + 1) * PART, :] = received[s, x, :PART, :]
        highest[...] = jnp.full(tall, LOW, jnp.float32)
        totals[...] = jnp.zeros(tall, jnp.float32)
        summed[...] = jnp.zeros(tall, jnp.float32)
        edge = (count - last * 8) * BLK
        bound = jnp.where(least < edge, 0, jnp.where((least < edge + BLK) & (own > 0), least - edge, NB))

        def score(i, masked):
            raw = nt(query[...], gathered(s, i, slice(0, HEAD)))
            if masked:
                raw = jnp.where(offset >= bound, raw, LOW)
            scores[i] = raw
            top = highest[...]
            for k in range(tiles):
                top = jnp.maximum(top, raw[:, k * HEAD : (k + 1) * HEAD])
            highest[...] = top

        def weigh(i, masked):
            top = highest[...]
            total = totals[...]
            weights = []
            for k in range(tiles):
                columns = slice(k * HEAD, (k + 1) * HEAD)
                exponent = jnp.exp2((scores[i, :, columns] - top) * SCALE2)
                if masked:
                    exponent = jnp.where(offset >= bound[:, columns], exponent, 0.0)
                total = total + exponent
                weights.append(exponent.astype(jnp.bfloat16))
            totals[...] = total
            summed[...] += nn(jnp.concatenate(weights, axis=1), gathered(s, i, slice(HEAD, 2 * HEAD)))

        @pl.loop(0, last)
        def _(i):
            score(i, False)

        score(last, True)
        high = jnp.max(highest[...], axis=1, keepdims=True)
        highest[...] = jnp.broadcast_to(high, tall)

        @pl.loop(0, last)
        def _(i):
            weigh(i, False)

        weigh(last, True)
        total = jnp.sum(totals[...], axis=1, keepdims=True)
        some = total > 0.0
        safe = jnp.where(some, total, 1.0)
        result = (summed[...] * (1.0 / safe)).astype(jnp.bfloat16)
        size = jnp.where(some, high * SCALE2 + jnp.log2(safe), LOW)
        for x in range(4):
            rows = slice(x * PART, (x + 1) * PART)
            out[s, x, :PART, :] = result[rows, :]
            flat = jnp.sum(jnp.where(eye, size[rows, :], 0.0), axis=0, keepdims=True)
            first = flat.astype(jnp.bfloat16).astype(jnp.float32)
            second = (flat - first).astype(jnp.bfloat16).astype(jnp.float32)
            third = flat - first - second
            stats = jnp.where(
                stat_row == 0, first, jnp.where(stat_row == 1, second, jnp.where(stat_row == 2, third, 0.0))
            )
            out[s, x, PART:, :] = stats.astype(jnp.bfloat16)


def join_kernel(parts, out, joined):
    eye = lax.broadcasted_iota(jnp.int32, (PART, HEAD), 0) == lax.broadcasted_iota(
        jnp.int32, (PART, HEAD), 1
    )
    column = lambda w: jnp.sum(jnp.where(eye, w, 0.0), axis=1, keepdims=True)
    tokens = PART // GROUP
    for g in range(8):
        sizes = [
            jnp.sum(parts[y, g, PART:, :].astype(jnp.float32), axis=0, keepdims=True)
            for y in range(2)
        ]
        top = jnp.maximum(sizes[0], sizes[1])
        shares = [jnp.exp2(size - top) for size in sizes]
        whole = 1.0 / (shares[0] + shares[1])
        joined[...] = sum(
            parts[y, g, :PART, :].astype(jnp.float32) * column(shares[y] * whole) for y in range(2)
        )
        for h in range(GROUP):
            at = (g * GROUP + h) * HEAD
            out[:, at : at + HEAD] = joined[pl.ds(h, tokens, stride=GROUP), :].astype(jnp.bfloat16)


def body(queries, keys, values, parent_block, slot_block):
    tokens = queries.shape[0]
    vmem = pl.BlockSpec(memory_space=pltpu.VMEM)
    smem = pl.BlockSpec(memory_space=pltpu.SMEM)
    plane = ("yh", "yl", "x")
    heads = lambda a: a.reshape(tokens, 8, -1, HEAD).transpose(1, 0, 2, 3).reshape(8, -1, HEAD)

    sent = jnp.concatenate([heads(queries), heads(keys), heads(values)], axis=1)
    wide = sent.shape[1]
    sent = jnp.broadcast_to(sent[None], (2, 8, wide, HEAD)).reshape(16, wide, HEAD)
    received = lax.all_to_all(sent, plane, split_axis=0, concat_axis=0, tiled=True)
    pairs = pl.pallas_call(
        unpack_kernel,
        out_shape=jax.ShapeDtypeStruct((8 * tokens, 2 * HEAD), jnp.bfloat16),
        in_specs=[vmem],
        out_specs=vmem,
        scratch_shapes=[pltpu.VMEM((8 * tokens, 2 * HEAD), jnp.float32)],
        name="unpack",
    )(received.reshape(2, 8, wide, HEAD))
    near = lax.all_gather(pairs, "z", axis=0, tiled=True)
    far = lax.ppermute(near, "c", [(0, 1), (1, 0)])

    table = pl.pallas_call(
        table_kernel,
        out_shape=jax.ShapeDtypeStruct((8, NB), jnp.int32),
        in_specs=[vmem, vmem],
        out_specs=vmem,
        name="table",
    )(parent_block.reshape(1, NB), slot_block.reshape(1, NB))

    parts = pl.pallas_call(
        attend_kernel,
        out_shape=jax.ShapeDtypeStruct((4, 4, PART + 16, HEAD), jnp.bfloat16),
        in_specs=[smem, vmem, vmem, vmem],
        out_specs=vmem,
        scratch_shapes=[
            pltpu.VMEM((SLOTS * BLK, 2 * HEAD), jnp.bfloat16),
            pltpu.VMEM((ROWS, HEAD), jnp.bfloat16),
            pltpu.VMEM((SLOTS // 8, ROWS, CHUNK), jnp.float32),
            pltpu.VMEM((ROWS, HEAD), jnp.float32),
            pltpu.VMEM((ROWS, HEAD), jnp.float32),
            pltpu.VMEM((ROWS, HEAD), jnp.float32),
        ],
        compiler_params=pltpu.CompilerParams(vmem_limit_bytes=32 * 1024 * 1024),
        name="attend",
    )(table, received.reshape(4, 4, wide, HEAD), near, far)

    parts = lax.all_to_all(
        parts.reshape(16, PART + 16, HEAD), plane, split_axis=0, concat_axis=0, tiled=True
    )
    return pl.pallas_call(
        join_kernel,
        out_shape=jax.ShapeDtypeStruct(queries.shape, queries.dtype),
        in_specs=[vmem],
        out_specs=vmem,
        scratch_shapes=[pltpu.VMEM((PART, HEAD), jnp.float32)],
        name="join",
    )(parts.reshape(2, 8, PART + 16, HEAD))


def solution(mesh):
    fine = Mesh(mesh.devices.reshape(2, Z, 2, 2, 4), ("yh", "z", "c", "yl", "x"))
    rows = P(("yh", "z", "c", "yl", "x"), None)
    return jax.shard_map(
        body,
        mesh=fine,
        in_specs=(rows, rows, rows, P(), P()),
        out_specs=rows,
        check_vma=False,
    )
```

```python
import math

import jax
import jax.numpy as jnp
from jax import lax
from jax.experimental import pallas as pl
from jax.experimental.pallas import tpu as pltpu
from jax.sharding import Mesh
from jax.sharding import PartitionSpec as P

GROUP = 8
HEAD = 128
BLK = 48
NB = 128
Z = 16
SLOTS = 64
CHUNK = 8 * BLK
ROWS = BLK * GROUP
PART = ROWS // 4
SCALE2 = math.log2(math.e) / math.sqrt(HEAD)
LOW = -1e30


def nn(a, b):
    return lax.dot_general(a, b, (((1,), (0,)), ((), ())), preferred_element_type=jnp.float32)


def nt(a, b):
    return lax.dot_general(a, b, (((1,), (1,)), ((), ())), preferred_element_type=jnp.float32)


def table_kernel(parent, slot, table):
    yh, z, c = lax.axis_index("yh"), lax.axis_index("z"), lax.axis_index("c")
    square = (NB, NB)
    row = lax.broadcasted_iota(jnp.int32, square, 0)
    column = lax.broadcasted_iota(jnp.int32, square, 1)
    one = lambda hit: jnp.where(hit, 1.0, 0.0).astype(jnp.bfloat16)
    reach_t = one((parent[...] == row) | (row == column))
    for _ in range(NB.bit_length() - 1):
        reach_t = one(nn(reach_t, reach_t) > 0.5)
    place = one(slot[...] == row)
    s = lax.broadcasted_iota(jnp.int32, (16, NB), 0)
    j = lax.broadcasted_iota(jnp.int32, (16, NB), 1)
    mine = (((s // 2) * Z + z) * 2 + c) * 2 + s % 2
    block = nt(one(j == mine), place).astype(jnp.bfloat16)
    reached = nt(block, reach_t).astype(jnp.bfloat16)
    by_slot = nn(reached, place).astype(jnp.bfloat16)
    core = jnp.where(column < SLOTS // 2, c, 1 - c)
    theirs = ((yh * Z + (column % (SLOTS // 2)) // 2) * 2 + core) * 2 + column % 2
    order = one((row == theirs) & (column < SLOTS))
    own = (s // 2 == yh) & (j == z * 2 + s % 2)
    taken = (nn(by_slot, order) > 0.5) & ~own
    before = nn(one(taken), one(row < column))
    at = jnp.where(taken, before, -1.0)
    number = j.astype(jnp.float32).astype(jnp.bfloat16)
    lists = jnp.zeros((16, NB), jnp.float32)
    for q in range(4):
        hit = one(at[q : q + 1, :] == row.astype(jnp.float32))
        lists = jnp.where(s == q, nt(number, hit), lists)
    counts = jnp.sum(jnp.where(taken, 1.0, 0.0), axis=1, keepdims=True)
    last = (s // 2 == yh) & (j.astype(jnp.float32) == counts)
    lists = jnp.where(last, (z * 2 + s % 2).astype(jnp.float32), lists)
    lists = lists[:4].astype(jnp.int32)
    table[...] = jnp.concatenate([lists, jnp.broadcast_to(counts[:4], (4, NB)).astype(jnp.int32)], axis=0)


def pack_kernel(queries, keys, values, sent, spread):
    tokens = PART // GROUP
    for g in range(8):
        for h in range(GROUP):
            at = (g * GROUP + h) * HEAD
            spread[pl.ds(h, tokens, stride=GROUP), :] = queries[:, at : at + HEAD].astype(jnp.float32)
        columns = slice(g * HEAD, (g + 1) * HEAD)
        spread[PART : PART + tokens, :] = keys[:, columns].astype(jnp.float32)
        spread[PART + tokens :, :] = values[:, columns].astype(jnp.float32)
        packed = spread[...].astype(jnp.bfloat16)
        sent[0, g] = packed
        sent[1, g] = packed


def unpack_kernel(received, pairs, spread):
    tokens = PART // GROUP
    for g in range(8):
        both = received[0, g, PART : PART + 2 * tokens, :].astype(jnp.float32)
        spread[g * tokens : (g + 1) * tokens, :HEAD] = both[:tokens]
        spread[g * tokens : (g + 1) * tokens, HEAD:] = both[tokens:]
    pairs[...] = spread[...].astype(jnp.bfloat16)


def attend_kernel(found, received, near, far, out, table, arrived, pairs, queries, scores, highest, totals, summed):
    yh = lax.axis_index("yh")
    half = SLOTS // 2 * BLK
    copy = pltpu.make_async_copy(found, table, arrived)
    copy.start()
    pairs[:half, :] = near[...]
    pairs[half:, :] = far[...]
    copy.wait()
    eye = lax.broadcasted_iota(jnp.int32, (PART, HEAD), 0) == lax.broadcasted_iota(
        jnp.int32, (PART, HEAD), 1
    )
    stat_row = lax.broadcasted_iota(jnp.int32, (16, HEAD), 0)
    tall = (ROWS, HEAD)
    tiles = CHUNK // HEAD
    least = lax.broadcasted_iota(jnp.int32, (1, CHUNK), 1)
    offset = lax.broadcasted_iota(jnp.int32, (ROWS, 1), 0) // GROUP
    last, bound = [], []
    for s in range(4):
        own = jnp.where(yh == s // 2, 1, 0)
        count = table[4 + s, 0]
        last.append(jnp.maximum(count + own - 1, 0) // 8)
        edge = (count - last[s] * 8) * BLK
        tail = jnp.where((least < edge + BLK) & (own > 0), least - edge, NB)
        bound.append(jnp.where(least < edge, 0, tail))

    def gathered(s, i, n, columns):
        places = [pl.multiple_of(table[s, i * 8 + t] * BLK, 16) for t in range(8 * n)]
        return jnp.concatenate([pairs[pl.ds(place, BLK), columns] for place in places], axis=0)

    def ready(s):
        for x in range(4):
            queries[s % 2][x * PART : (x + 1) * PART, :] = received[s, x, :PART, :]
        highest[s % 2][...] = jnp.full(tall, LOW, jnp.float32)

    def score(s, i, n, masked):
        raw = nt(queries[s % 2][...], gathered(s, i, n, slice(0, HEAD)))
        top = highest[s % 2][...]
        for j in range(n):
            part = raw[:, j * CHUNK : (j + 1) * CHUNK]
            if masked and j == n - 1:
                part = jnp.where(offset >= bound[s], part, LOW)
            scores[s % 2][i + j] = part
            for k in range(tiles):
                top = jnp.maximum(top, part[:, k * HEAD : (k + 1) * HEAD])
        highest[s % 2][...] = top

    def weigh(s, i, n, masked):
        top = highest[s % 2][...]
        total = totals[...]
        weights = []
        for j in range(n):
            for k in range(tiles):
                columns = slice(k * HEAD, (k + 1) * HEAD)
                exponent = jnp.exp2((scores[s % 2][i + j, :, columns] - top) * SCALE2)
                if masked and j == n - 1:
                    exponent = jnp.where(offset >= bound[s][:, columns], exponent, 0.0)
                total = total + exponent
                weights.append(exponent.astype(jnp.bfloat16))
        totals[...] = total
        summed[...] += nn(jnp.concatenate(weights, axis=1), gathered(s, i, n, slice(HEAD, 2 * HEAD)))

    def run(*work):
        whole = [last[s] // 2 for _, s in work]
        together = whole[0] if len(work) == 1 else jnp.minimum(*whole)

        @pl.loop(0, together)
        def _(i):
            for step, s in work:
                step(s, 2 * i, 2, False)

        if len(work) > 1:
            for (step, s), end in zip(work, whole):

                @pl.loop(together, end)
                def _(i, step=step, s=s):
                    step(s, 2 * i, 2, False)

        for case in range(2 ** len(work)):
            odd = [case >> w & 1 for w in range(len(work))]
            here = [last[s] % 2 == odd[w] for w, (_, s) in enumerate(work)]

            @pl.when(here[0] if len(work) == 1 else here[0] & here[1])
            def _(odd=odd):
                for (step, s), extra in zip(work, odd):
                    step(s, last[s] - extra, 1 + extra, True)

    ready(0)
    run((score, 0))
    for s in range(4):
        high = jnp.max(highest[s % 2][...], axis=1, keepdims=True)
        highest[s % 2][...] = jnp.broadcast_to(high, tall)
        totals[...] = jnp.zeros(tall, jnp.float32)
        summed[...] = jnp.zeros(tall, jnp.float32)
        if s < 3:
            ready(s + 1)
            run((weigh, s), (score, s + 1))
        else:
            run((weigh, s))
        total = jnp.sum(totals[...], axis=1, keepdims=True)
        some = total > 0.0
        safe = jnp.where(some, total, 1.0)
        result = (summed[...] * (1.0 / safe)).astype(jnp.bfloat16)
        size = jnp.where(some, high * SCALE2 + jnp.log2(safe), LOW)
        for x in range(4):
            rows = slice(x * PART, (x + 1) * PART)
            out[s, x, :PART, :] = result[rows, :]
            flat = jnp.sum(jnp.where(eye, size[rows, :], 0.0), axis=0, keepdims=True)
            first = flat.astype(jnp.bfloat16).astype(jnp.float32)
            second = (flat - first).astype(jnp.bfloat16).astype(jnp.float32)
            third = flat - first - second
            stats = jnp.where(
                stat_row == 0, first, jnp.where(stat_row == 1, second, jnp.where(stat_row == 2, third, 0.0))
            )
            out[s, x, PART:, :] = stats.astype(jnp.bfloat16)


def join_kernel(parts, out, joined):
    eye = lax.broadcasted_iota(jnp.int32, (PART, HEAD), 0) == lax.broadcasted_iota(
        jnp.int32, (PART, HEAD), 1
    )
    column = lambda w: jnp.sum(jnp.where(eye, w, 0.0), axis=1, keepdims=True)
    tokens = PART // GROUP
    for g in range(8):
        sizes = [
            jnp.sum(parts[y, g, PART:, :].astype(jnp.float32), axis=0, keepdims=True)
            for y in range(2)
        ]
        top = jnp.maximum(sizes[0], sizes[1])
        shares = [jnp.exp2(size - top) for size in sizes]
        whole = 1.0 / (shares[0] + shares[1])
        joined[...] = sum(
            parts[y, g, :PART, :].astype(jnp.float32) * column(shares[y] * whole) for y in range(2)
        )
        for h in range(GROUP):
            at = (g * GROUP + h) * HEAD
            out[:, at : at + HEAD] = joined[pl.ds(h, tokens, stride=GROUP), :].astype(jnp.bfloat16)


def body(queries, keys, values, parent_block, slot_block):
    tokens = queries.shape[0]
    vmem = pl.BlockSpec(memory_space=pltpu.VMEM)
    plane = ("yh", "yl", "x")
    wide = PART + 2 * tokens
    sent = pl.pallas_call(
        pack_kernel,
        out_shape=jax.ShapeDtypeStruct((2, 8, wide, HEAD), jnp.bfloat16),
        in_specs=[vmem, vmem, vmem],
        out_specs=vmem,
        scratch_shapes=[pltpu.VMEM((wide, HEAD), jnp.float32)],
        name="pack",
    )(queries, keys, values).reshape(16, wide, HEAD)
    received = lax.all_to_all(sent, plane, split_axis=0, concat_axis=0, tiled=True)
    pairs = pl.pallas_call(
        unpack_kernel,
        out_shape=jax.ShapeDtypeStruct((8 * tokens, 2 * HEAD), jnp.bfloat16),
        grid=(1,),
        in_specs=[pl.BlockSpec((1, 8, wide, HEAD), lambda i: (lax.axis_index("yh"), 0, 0, 0))],
        out_specs=pl.BlockSpec((8 * tokens, 2 * HEAD), lambda i: (0, 0)),
        scratch_shapes=[pltpu.VMEM((8 * tokens, 2 * HEAD), jnp.float32)],
        name="unpack",
    )(received.reshape(2, 8, wide, HEAD))
    near = lax.all_gather(pairs, "z", axis=0, tiled=True)
    far = lax.ppermute(near, "c", [(0, 1), (1, 0)])

    table = pl.pallas_call(
        table_kernel,
        out_shape=jax.ShapeDtypeStruct((8, NB), jnp.int32),
        in_specs=[vmem, vmem],
        out_specs=vmem,
        name="table",
    )(parent_block.reshape(1, NB), slot_block.reshape(1, NB))

    parts = pl.pallas_call(
        attend_kernel,
        out_shape=jax.ShapeDtypeStruct((4, 4, PART + 16, HEAD), jnp.bfloat16),
        in_specs=[pl.BlockSpec(memory_space=pl.ANY), vmem, vmem, vmem],
        out_specs=vmem,
        scratch_shapes=[
            pltpu.SMEM((8, NB), jnp.int32),
            pltpu.SemaphoreType.DMA,
            pltpu.VMEM((SLOTS * BLK, 2 * HEAD), jnp.bfloat16),
            [pltpu.VMEM((ROWS, HEAD), jnp.bfloat16)] * 2,
            [pltpu.VMEM((SLOTS // 8, ROWS, CHUNK), jnp.float32)] * 2,
            [pltpu.VMEM((ROWS, HEAD), jnp.float32)] * 2,
            pltpu.VMEM((ROWS, HEAD), jnp.float32),
            pltpu.VMEM((ROWS, HEAD), jnp.float32),
        ],
        compiler_params=pltpu.CompilerParams(vmem_limit_bytes=32 * 1024 * 1024),
        name="attend",
    )(table, received.reshape(4, 4, wide, HEAD), near, far)

    parts = lax.all_to_all(
        parts.reshape(16, PART + 16, HEAD), plane, split_axis=0, concat_axis=0, tiled=True
    )
    return pl.pallas_call(
        join_kernel,
        out_shape=jax.ShapeDtypeStruct(queries.shape, queries.dtype),
        in_specs=[vmem],
        out_specs=vmem,
        scratch_shapes=[pltpu.VMEM((PART, HEAD), jnp.float32)],
        name="join",
    )(parts.reshape(2, 8, PART + 16, HEAD))


def solution(mesh):
    fine = Mesh(mesh.devices.reshape(2, Z, 2, 2, 4), ("yh", "z", "c", "yl", "x"))
    rows = P(("yh", "z", "c", "yl", "x"), None)
    return jax.shard_map(
        body,
        mesh=fine,
        in_specs=(rows, rows, rows, P(), P()),
        out_specs=rows,
        check_vma=False,
    )
```

```python
import math

import jax
import jax.numpy as jnp
from jax import lax
from jax.experimental import pallas as pl
from jax.experimental.pallas import tpu as pltpu
from jax.sharding import Mesh
from jax.sharding import PartitionSpec as P

GROUP = 8
HEAD = 128
BLK = 48
NB = 128
Z = 16
SLOTS = 64
CHUNK = 8 * BLK
ROWS = BLK * GROUP
PART = ROWS // 4
SCALE2 = math.log2(math.e) / math.sqrt(HEAD)
LOW = -1e30


def nn(a, b):
    return lax.dot_general(a, b, (((1,), (0,)), ((), ())), preferred_element_type=jnp.float32)


def nt(a, b):
    return lax.dot_general(a, b, (((1,), (1,)), ((), ())), preferred_element_type=jnp.float32)


def table_kernel(parent, slot, table):
    yh, z, c = lax.axis_index("yh"), lax.axis_index("z"), lax.axis_index("c")
    square = (NB, NB)
    row = lax.broadcasted_iota(jnp.int32, square, 0)
    column = lax.broadcasted_iota(jnp.int32, square, 1)
    one = lambda hit: jnp.where(hit, 1.0, 0.0).astype(jnp.bfloat16)
    reach_t = one((parent[...] == row) | (row == column))
    for _ in range(NB.bit_length() - 2):
        reach_t = one(nn(reach_t, reach_t) > 0.5)
    place = one(slot[...] == row)
    s = lax.broadcasted_iota(jnp.int32, (16, NB), 0)
    j = lax.broadcasted_iota(jnp.int32, (16, NB), 1)
    mine = (((s // 2) * Z + z) * 2 + c) * 2 + s % 2
    block = nt(one(j == mine), place).astype(jnp.bfloat16)
    reached = one(nt(one(nt(block, reach_t) > 0.5), reach_t) > 0.5)
    core = jnp.where(column < SLOTS // 2, c, 1 - c)
    theirs = ((yh * Z + (column % (SLOTS // 2)) // 2) * 2 + core) * 2 + column % 2
    order = one((row == theirs) & (column < SLOTS))
    held = nn(place, order).astype(jnp.bfloat16)
    own = (s // 2 == yh) & (j == z * 2 + s % 2)
    taken = (nn(reached, held) > 0.5) & ~own
    before = nn(one(taken), one(row < column))
    at = jnp.where(taken, before, -1.0)
    number = j.astype(jnp.float32).astype(jnp.bfloat16)
    lists = jnp.zeros((16, NB), jnp.float32)
    for q in range(4):
        hit = one(at[q : q + 1, :] == row.astype(jnp.float32))
        lists = jnp.where(s == q, nt(number, hit), lists)
    counts = jnp.sum(jnp.where(taken, 1.0, 0.0), axis=1, keepdims=True)
    last = (s // 2 == yh) & (j.astype(jnp.float32) == counts)
    lists = jnp.where(last, (z * 2 + s % 2).astype(jnp.float32), lists)
    lists = lists[:4].astype(jnp.int32)
    table[...] = jnp.concatenate([lists, jnp.broadcast_to(counts[:4], (4, NB)).astype(jnp.int32)], axis=0)


def pack_kernel(queries, keys, values, sent, spread):
    tokens = PART // GROUP
    for g in range(8):
        for h in range(GROUP):
            at = (g * GROUP + h) * HEAD
            rows = pl.ds(h, tokens, stride=GROUP)
            spread[g, rows, :] = queries[:, at : at + HEAD].astype(jnp.float32)
        columns = slice(g * HEAD, (g + 1) * HEAD)
        spread[g, PART : PART + tokens, :] = keys[:, columns].astype(jnp.float32)
        spread[g, PART + tokens :, :] = values[:, columns].astype(jnp.float32)
    for g in range(8):
        packed = spread[g].astype(jnp.bfloat16)
        sent[0, g] = packed
        sent[1, g] = packed


def unpack_kernel(received, pairs, spread):
    tokens = PART // GROUP
    for g in range(8):
        both = received[0, g, PART : PART + 2 * tokens, :].astype(jnp.float32)
        spread[g * tokens : (g + 1) * tokens, :HEAD] = both[:tokens]
        spread[g * tokens : (g + 1) * tokens, HEAD:] = both[tokens:]
    pairs[...] = spread[...].astype(jnp.bfloat16)


def attend_kernel(found, received, near, far, out, table, arrived, pairs, queries, scores, highest, totals, summed):
    yh = lax.axis_index("yh")
    half = SLOTS // 2 * BLK
    copy = pltpu.make_async_copy(found, table, arrived)
    copy.start()
    pairs[:half, :] = near[...]
    pairs[half:, :] = far[...]
    copy.wait()
    eye = lax.broadcasted_iota(jnp.int32, (PART, HEAD), 0) == lax.broadcasted_iota(
        jnp.int32, (PART, HEAD), 1
    )
    stat_row = lax.broadcasted_iota(jnp.int32, (16, HEAD), 0)
    tall = (ROWS, HEAD)
    tiles = CHUNK // HEAD
    least = lax.broadcasted_iota(jnp.int32, (1, CHUNK), 1)
    offset = lax.broadcasted_iota(jnp.int32, (ROWS, 1), 0) // GROUP
    last, bound = [], []
    for s in range(4):
        own = jnp.where(yh == s // 2, 1, 0)
        count = table[4 + s, 0]
        last.append(jnp.maximum(count + own - 1, 0) // 8)
        edge = (count - last[s] * 8) * BLK
        tail = jnp.where((least < edge + BLK) & (own > 0), least - edge, NB)
        bound.append(jnp.where(least < edge, 0, tail))

    def gathered(s, i, n, columns):
        places = [pl.multiple_of(table[s, i * 8 + t] * BLK, 16) for t in range(8 * n)]
        return jnp.concatenate([pairs[pl.ds(place, BLK), columns] for place in places], axis=0)

    def ready(s):
        for x in range(4):
            queries[s % 2][x * PART : (x + 1) * PART, :] = received[s // 2, s % 2 * 4 + x, :PART, :]
        highest[s % 2][...] = jnp.full(tall, LOW, jnp.float32)

    def score(s, i, n, masked):
        raw = nt(queries[s % 2][...], gathered(s, i, n, slice(0, HEAD)))
        top = highest[s % 2][...]
        for j in range(n):
            part = raw[:, j * CHUNK : (j + 1) * CHUNK]
            if masked and j == n - 1:
                part = jnp.where(offset >= bound[s], part, LOW)
            scores[s % 2][i + j] = part
            for k in range(tiles):
                top = jnp.maximum(top, part[:, k * HEAD : (k + 1) * HEAD])
        highest[s % 2][...] = top

    def weigh(s, i, n, masked):
        top = highest[s % 2][...]
        total = totals[...]
        weights = []
        for j in range(n):
            for k in range(tiles):
                columns = slice(k * HEAD, (k + 1) * HEAD)
                exponent = jnp.exp2((scores[s % 2][i + j, :, columns] - top) * SCALE2)
                if masked and j == n - 1:
                    exponent = jnp.where(offset >= bound[s][:, columns], exponent, 0.0)
                total = total + exponent
                weights.append(exponent.astype(jnp.bfloat16))
        totals[...] = total
        summed[...] += nn(jnp.concatenate(weights, axis=1), gathered(s, i, n, slice(HEAD, 2 * HEAD)))

    def run(*work):
        whole = [last[s] // 2 for _, s in work]
        together = whole[0] if len(work) == 1 else jnp.minimum(*whole)

        @pl.loop(0, together)
        def _(i):
            for step, s in work:
                step(s, 2 * i, 2, False)

        if len(work) > 1:
            for (step, s), end in zip(work, whole):

                @pl.loop(together, end)
                def _(i, step=step, s=s):
                    step(s, 2 * i, 2, False)

        for case in range(2 ** len(work)):
            odd = [case >> w & 1 for w in range(len(work))]
            here = [last[s] % 2 == odd[w] for w, (_, s) in enumerate(work)]

            @pl.when(here[0] if len(work) == 1 else here[0] & here[1])
            def _(odd=odd):
                for (step, s), extra in zip(work, odd):
                    step(s, last[s] - extra, 1 + extra, True)

    ready(0)
    run((score, 0))
    for s in range(4):
        high = jnp.max(highest[s % 2][...], axis=1, keepdims=True)
        highest[s % 2][...] = jnp.broadcast_to(high, tall)
        totals[...] = jnp.zeros(tall, jnp.float32)
        summed[...] = jnp.zeros(tall, jnp.float32)
        if s < 3:
            ready(s + 1)
            run((weigh, s), (score, s + 1))
        else:
            run((weigh, s))
        total = jnp.sum(totals[...], axis=1, keepdims=True)
        some = total > 0.0
        safe = jnp.where(some, total, 1.0)
        result = (summed[...] * (1.0 / safe)).astype(jnp.bfloat16)
        size = jnp.where(some, high * SCALE2 + jnp.log2(safe), LOW)
        for x in range(4):
            rows = slice(x * PART, (x + 1) * PART)
            out[s, x, :PART, :] = result[rows, :]
            flat = jnp.sum(jnp.where(eye, size[rows, :], 0.0), axis=0, keepdims=True)
            first = flat.astype(jnp.bfloat16).astype(jnp.float32)
            second = (flat - first).astype(jnp.bfloat16).astype(jnp.float32)
            third = flat - first - second
            stats = jnp.where(
                stat_row == 0, first, jnp.where(stat_row == 1, second, jnp.where(stat_row == 2, third, 0.0))
            )
            out[s, x, PART:, :] = stats.astype(jnp.bfloat16)


def join_kernel(parts, out, joined):
    eye = lax.broadcasted_iota(jnp.int32, (PART, HEAD), 0) == lax.broadcasted_iota(
        jnp.int32, (PART, HEAD), 1
    )
    tokens = PART // GROUP
    for g in range(8):
        sizes = [
            jnp.sum(parts[y, g, PART:, :].astype(jnp.float32), axis=0, keepdims=True)
            for y in range(2)
        ]
        top = jnp.maximum(sizes[0], sizes[1])
        shares = [jnp.exp2(size - top) for size in sizes]
        first = shares[0] / (shares[0] + shares[1])
        first = jnp.sum(jnp.where(eye, first, 0.0), axis=1, keepdims=True)
        one, other = [parts[y, g, :PART, :].astype(jnp.float32) for y in range(2)]
        joined[g * PART : (g + 1) * PART, :] = other + (one - other) * first
    for g in range(8):
        for h in range(GROUP):
            at = (g * GROUP + h) * HEAD
            rows = pl.ds(g * PART + h, tokens, stride=GROUP)
            out[:, at : at + HEAD] = joined[rows, :].astype(jnp.bfloat16)


def body(queries, keys, values, parent_block, slot_block):
    tokens = queries.shape[0]
    vmem = pl.BlockSpec(memory_space=pltpu.VMEM)
    plane = ("yh", "yl", "x")
    wide = PART + 2 * tokens
    sent = pl.pallas_call(
        pack_kernel,
        out_shape=pltpu.VMEM((2, 8, wide, HEAD), jnp.bfloat16),
        in_specs=[vmem, vmem, vmem],
        out_specs=vmem,
        scratch_shapes=[pltpu.VMEM((8, wide, HEAD), jnp.float32)],
        name="pack",
    )(queries, keys, values).reshape(16, wide, HEAD)
    received = lax.all_to_all(sent, plane, split_axis=0, concat_axis=0, tiled=True)
    received = pltpu.with_memory_space_constraint(received.reshape(2, 8, wide, HEAD), pltpu.VMEM)
    pairs = pl.pallas_call(
        unpack_kernel,
        out_shape=pltpu.VMEM((8 * tokens, 2 * HEAD), jnp.bfloat16),
        grid=(1,),
        in_specs=[pl.BlockSpec((1, 8, wide, HEAD), lambda i: (lax.axis_index("yh"), 0, 0, 0))],
        out_specs=pl.BlockSpec((8 * tokens, 2 * HEAD), lambda i: (0, 0)),
        scratch_shapes=[pltpu.VMEM((8 * tokens, 2 * HEAD), jnp.float32)],
        name="unpack",
    )(received)
    near = lax.all_gather(pairs, "z", axis=0, tiled=True)
    far = lax.ppermute(near, "c", [(0, 1), (1, 0)])

    table = pl.pallas_call(
        table_kernel,
        out_shape=pltpu.VMEM((8, NB), jnp.int32),
        in_specs=[vmem, vmem],
        out_specs=vmem,
        name="table",
    )(parent_block.reshape(1, NB), slot_block.reshape(1, NB))

    parts = pl.pallas_call(
        attend_kernel,
        out_shape=pltpu.VMEM((4, 4, PART + 16, HEAD), jnp.bfloat16),
        in_specs=[pl.BlockSpec(memory_space=pl.ANY), vmem, vmem, vmem],
        out_specs=vmem,
        scratch_shapes=[
            pltpu.SMEM((8, NB), jnp.int32),
            pltpu.SemaphoreType.DMA,
            pltpu.VMEM((SLOTS * BLK, 2 * HEAD), jnp.bfloat16),
            [pltpu.VMEM((ROWS, HEAD), jnp.bfloat16)] * 2,
            [pltpu.VMEM((SLOTS // 8, ROWS, CHUNK), jnp.float32)] * 2,
            [pltpu.VMEM((ROWS, HEAD), jnp.float32)] * 2,
            pltpu.VMEM((ROWS, HEAD), jnp.float32),
            pltpu.VMEM((ROWS, HEAD), jnp.float32),
        ],
        compiler_params=pltpu.CompilerParams(vmem_limit_bytes=32 * 1024 * 1024),
        name="attend",
    )(table, received, near, far)

    parts = lax.all_to_all(
        parts.reshape(16, PART + 16, HEAD), plane, split_axis=0, concat_axis=0, tiled=True
    )
    parts = pltpu.with_memory_space_constraint(parts.reshape(2, 8, PART + 16, HEAD), pltpu.VMEM)
    return pl.pallas_call(
        join_kernel,
        out_shape=jax.ShapeDtypeStruct(queries.shape, queries.dtype),
        in_specs=[vmem],
        out_specs=vmem,
        scratch_shapes=[pltpu.VMEM((8 * PART, HEAD), jnp.float32)],
        name="join",
    )(parts)


def solution(mesh):
    fine = Mesh(mesh.devices.reshape(2, Z, 2, 2, 4), ("yh", "z", "c", "yl", "x"))
    rows = P(("yh", "z", "c", "yl", "x"), None)
    return jax.shard_map(
        body,
        mesh=fine,
        in_specs=(rows, rows, rows, P(), P()),
        out_specs=rows,
        check_vma=False,
    )
```

```python
import math

import jax
import jax.numpy as jnp
from jax import lax
from jax.experimental import pallas as pl
from jax.experimental.pallas import tpu as pltpu
from jax.sharding import Mesh
from jax.sharding import PartitionSpec as P

GROUP = 8
HEAD = 128
BLK = 48
NB = 128
Z = 16
SLOTS = 64
CHUNK = 8 * BLK
ROWS = BLK * GROUP
PART = ROWS // 4
SCALE2 = math.log2(math.e) / math.sqrt(HEAD)
LOW = -1e30


def nn(a, b):
    return lax.dot_general(a, b, (((1,), (0,)), ((), ())), preferred_element_type=jnp.float32)


def nt(a, b):
    return lax.dot_general(a, b, (((1,), (1,)), ((), ())), preferred_element_type=jnp.float32)


def table_kernel(parent, slot, table):
    yh, z, c = lax.axis_index("yh"), lax.axis_index("z"), lax.axis_index("c")
    square = (NB, NB)
    row = lax.broadcasted_iota(jnp.int32, square, 0)
    column = lax.broadcasted_iota(jnp.int32, square, 1)
    one = lambda hit: jnp.where(hit, 1.0, 0.0).astype(jnp.bfloat16)
    reach_t = one((parent[...] == row) | (row == column))
    for _ in range(NB.bit_length() - 2):
        reach_t = one(nn(reach_t, reach_t) > 0.5)
    place = one(slot[...] == row)
    s = lax.broadcasted_iota(jnp.int32, (16, NB), 0)
    j = lax.broadcasted_iota(jnp.int32, (16, NB), 1)
    mine = (((s // 2) * Z + z) * 2 + c) * 2 + s % 2
    block = nt(one(j == mine), place).astype(jnp.bfloat16)
    reached = one(nt(one(nt(block, reach_t) > 0.5), reach_t) > 0.5)
    core = jnp.where(column < SLOTS // 2, c, 1 - c)
    theirs = ((yh * Z + (column % (SLOTS // 2)) // 2) * 2 + core) * 2 + column % 2
    order = one((row == theirs) & (column < SLOTS))
    held = nn(place, order).astype(jnp.bfloat16)
    own = (s // 2 == yh) & (j == z * 2 + s % 2)
    taken = (nn(reached, held) > 0.5) & ~own
    before = nn(one(taken), one(row < column))
    at = jnp.where(taken, before, -1.0)
    number = j.astype(jnp.float32).astype(jnp.bfloat16)
    lists = jnp.zeros((16, NB), jnp.float32)
    for q in range(4):
        hit = one(at[q : q + 1, :] == row.astype(jnp.float32))
        lists = jnp.where(s == q, nt(number, hit), lists)
    counts = jnp.sum(jnp.where(taken, 1.0, 0.0), axis=1, keepdims=True)
    last = (s // 2 == yh) & (j.astype(jnp.float32) == counts)
    lists = jnp.where(last, (z * 2 + s % 2).astype(jnp.float32), lists)
    lists = lists[:4].astype(jnp.int32)
    table[...] = jnp.concatenate([lists, jnp.broadcast_to(counts[:4], (4, NB)).astype(jnp.int32)], axis=0)


def pack_kernel(queries, keys, values, sent, spread):
    tokens = PART // GROUP
    for g in range(8):
        for h in range(GROUP):
            at = (g * GROUP + h) * HEAD
            rows = pl.ds(h, tokens, stride=GROUP)
            spread[g, rows, :] = queries[:, at : at + HEAD].astype(jnp.float32)
        columns = slice(g * HEAD, (g + 1) * HEAD)
        spread[g, PART : PART + tokens, :] = keys[:, columns].astype(jnp.float32)
        spread[g, PART + tokens :, :] = values[:, columns].astype(jnp.float32)
    for g in range(8):
        packed = spread[g].astype(jnp.bfloat16)
        sent[0, g] = packed
        sent[1, g] = packed


def unpack_kernel(received, pairs, spread):
    tokens = PART // GROUP
    for g in range(8):
        both = received[0, g, PART : PART + 2 * tokens, :].astype(jnp.float32)
        spread[g * tokens : (g + 1) * tokens, :HEAD] = both[:tokens]
        spread[g * tokens : (g + 1) * tokens, HEAD:] = both[tokens:]
    pairs[...] = spread[...].astype(jnp.bfloat16)


def attend_kernel(found, received, near, far, out, table, arrived, pairs, queries, scores, highest, totals, summed):
    yh = lax.axis_index("yh")
    half = SLOTS // 2 * BLK
    copy = pltpu.make_async_copy(found, table, arrived)
    copy.start()
    pairs[:half, :] = near[...]
    pairs[half:, :] = far[...]
    copy.wait()
    eye = lax.broadcasted_iota(jnp.int32, (PART, HEAD), 0) == lax.broadcasted_iota(
        jnp.int32, (PART, HEAD), 1
    )
    stat_row = lax.broadcasted_iota(jnp.int32, (8, HEAD), 0)
    tall = (ROWS, HEAD)
    tiles = CHUNK // HEAD
    least = lax.broadcasted_iota(jnp.int32, (1, CHUNK), 1)
    offset = lax.broadcasted_iota(jnp.int32, (ROWS, 1), 0) // GROUP
    last, bound = [], []
    for s in range(4):
        own = jnp.where(yh == s // 2, 1, 0)
        count = table[4 + s, 0]
        last.append(jnp.maximum(count + own - 1, 0) // 8)
        edge = (count - last[s] * 8) * BLK
        tail = jnp.where((least < edge + BLK) & (own > 0), least - edge, NB)
        bound.append(jnp.where(least < edge, 0, tail))

    def gathered(s, i, n, columns):
        places = [pl.multiple_of(table[s, i * 8 + t] * BLK, 16) for t in range(8 * n)]
        return jnp.concatenate([pairs[pl.ds(place, BLK), columns] for place in places], axis=0)

    def ready(s):
        for x in range(4):
            queries[s % 2][x * PART : (x + 1) * PART, :] = received[s // 2, s % 2 * 4 + x, :PART, :]
        highest[s % 2][...] = jnp.full(tall, LOW, jnp.float32)

    def score(s, i, n, masked):
        raw = nt(queries[s % 2][...], gathered(s, i, n, slice(0, HEAD)))
        top = highest[s % 2][...]
        for j in range(n):
            part = raw[:, j * CHUNK : (j + 1) * CHUNK]
            if masked and j == n - 1:
                part = jnp.where(offset >= bound[s], part, LOW)
            scores[s % 2][i + j] = part
            for k in range(tiles):
                top = jnp.maximum(top, part[:, k * HEAD : (k + 1) * HEAD])
        highest[s % 2][...] = top

    def weigh(s, i, n, masked):
        top = highest[s % 2][...]
        total = totals[...]
        weights = []
        for j in range(n):
            for k in range(tiles):
                columns = slice(k * HEAD, (k + 1) * HEAD)
                exponent = jnp.exp2((scores[s % 2][i + j, :, columns] - top) * SCALE2)
                if masked and j == n - 1:
                    exponent = jnp.where(offset >= bound[s][:, columns], exponent, 0.0)
                total = total + exponent
                weights.append(exponent.astype(jnp.bfloat16))
        totals[...] = total
        summed[...] += nn(jnp.concatenate(weights, axis=1), gathered(s, i, n, slice(HEAD, 2 * HEAD)))

    def run(*work):
        whole = [last[s] // 2 for _, s in work]
        together = whole[0] if len(work) == 1 else jnp.minimum(*whole)

        @pl.loop(0, together)
        def _(i):
            for step, s in work:
                step(s, 2 * i, 2, False)

        if len(work) > 1:
            for (step, s), end in zip(work, whole):

                @pl.loop(together, end)
                def _(i, step=step, s=s):
                    step(s, 2 * i, 2, False)

        for case in range(2 ** len(work)):
            odd = [case >> w & 1 for w in range(len(work))]
            here = [last[s] % 2 == odd[w] for w, (_, s) in enumerate(work)]

            @pl.when(here[0] if len(work) == 1 else here[0] & here[1])
            def _(odd=odd):
                for (step, s), extra in zip(work, odd):
                    step(s, last[s] - extra, 1 + extra, True)

    ready(0)
    run((score, 0))
    for s in range(4):
        high = jnp.max(highest[s % 2][...], axis=1, keepdims=True)
        highest[s % 2][...] = jnp.broadcast_to(high, tall)
        totals[...] = jnp.zeros(tall, jnp.float32)
        summed[...] = jnp.zeros(tall, jnp.float32)
        if s < 3:
            ready(s + 1)
            run((weigh, s), (score, s + 1))
        else:
            run((weigh, s))
        total = jnp.sum(totals[...], axis=1, keepdims=True)
        some = total > 0.0
        safe = jnp.where(some, total, 1.0)
        result = (summed[...] * (1.0 / safe)).astype(jnp.bfloat16)
        size = jnp.where(some, high * SCALE2 + jnp.log2(safe), LOW)
        for x in range(4):
            rows = slice(x * PART, (x + 1) * PART)
            out[s, x, :PART, :] = result[rows, :]
            flat = jnp.sum(jnp.where(eye, size[rows, :], 0.0), axis=0, keepdims=True)
            first = flat.astype(jnp.bfloat16).astype(jnp.float32)
            second = (flat - first).astype(jnp.bfloat16).astype(jnp.float32)
            third = flat - first - second
            stats = jnp.where(
                stat_row == 0, first, jnp.where(stat_row == 1, second, jnp.where(stat_row == 2, third, 0.0))
            )
            out[s, x, PART:, :] = stats.astype(jnp.bfloat16)


def join_kernel(parts, out, joined):
    eye = lax.broadcasted_iota(jnp.int32, (PART, HEAD), 0) == lax.broadcasted_iota(
        jnp.int32, (PART, HEAD), 1
    )
    tokens = PART // GROUP
    for g in range(8):
        sizes = [
            jnp.sum(parts[y, g, PART:, :].astype(jnp.float32), axis=0, keepdims=True)
            for y in range(2)
        ]
        top = jnp.maximum(sizes[0], sizes[1])
        shares = [jnp.exp2(size - top) for size in sizes]
        first = shares[0] / (shares[0] + shares[1])
        first = jnp.sum(jnp.where(eye, first, 0.0), axis=1, keepdims=True)
        one, other = [parts[y, g, :PART, :].astype(jnp.float32) for y in range(2)]
        joined[g * PART : (g + 1) * PART, :] = other + (one - other) * first
    for g in range(8):
        for h in range(GROUP):
            at = (g * GROUP + h) * HEAD
            rows = pl.ds(g * PART + h, tokens, stride=GROUP)
            out[:, at : at + HEAD] = joined[rows, :].astype(jnp.bfloat16)


def body(queries, keys, values, parent_block, slot_block):
    tokens = queries.shape[0]
    vmem = pl.BlockSpec(memory_space=pltpu.VMEM)
    plane = ("yh", "yl", "x")
    wide = PART + 2 * tokens
    sent = pl.pallas_call(
        pack_kernel,
        out_shape=pltpu.VMEM((2, 8, wide, HEAD), jnp.bfloat16),
        in_specs=[vmem, vmem, vmem],
        out_specs=vmem,
        scratch_shapes=[pltpu.VMEM((8, wide, HEAD), jnp.float32)],
        name="pack",
    )(queries, keys, values).reshape(16, wide, HEAD)
    received = lax.all_to_all(sent, plane, split_axis=0, concat_axis=0, tiled=True)
    received = pltpu.with_memory_space_constraint(received.reshape(2, 8, wide, HEAD), pltpu.VMEM)
    pairs = pl.pallas_call(
        unpack_kernel,
        out_shape=pltpu.VMEM((8 * tokens, 2 * HEAD), jnp.bfloat16),
        grid=(1,),
        in_specs=[pl.BlockSpec((1, 8, wide, HEAD), lambda i: (lax.axis_index("yh"), 0, 0, 0))],
        out_specs=pl.BlockSpec((8 * tokens, 2 * HEAD), lambda i: (0, 0)),
        scratch_shapes=[pltpu.VMEM((8 * tokens, 2 * HEAD), jnp.float32)],
        name="unpack",
    )(received)
    near = lax.all_gather(pairs, "z", axis=0, tiled=True)
    far = lax.ppermute(near, "c", [(0, 1), (1, 0)])

    table = pl.pallas_call(
        table_kernel,
        out_shape=pltpu.VMEM((8, NB), jnp.int32),
        in_specs=[vmem, vmem],
        out_specs=vmem,
        name="table",
    )(parent_block.reshape(1, NB), slot_block.reshape(1, NB))

    parts = pl.pallas_call(
        attend_kernel,
        out_shape=pltpu.VMEM((4, 4, PART + 8, HEAD), jnp.bfloat16),
        in_specs=[pl.BlockSpec(memory_space=pl.ANY), vmem, vmem, vmem],
        out_specs=vmem,
        scratch_shapes=[
            pltpu.SMEM((8, NB), jnp.int32),
            pltpu.SemaphoreType.DMA,
            pltpu.VMEM((SLOTS * BLK, 2 * HEAD), jnp.bfloat16),
            [pltpu.VMEM((ROWS, HEAD), jnp.bfloat16)] * 2,
            [pltpu.VMEM((SLOTS // 8, ROWS, CHUNK), jnp.float32)] * 2,
            [pltpu.VMEM((ROWS, HEAD), jnp.float32)] * 2,
            pltpu.VMEM((ROWS, HEAD), jnp.float32),
            pltpu.VMEM((ROWS, HEAD), jnp.float32),
        ],
        compiler_params=pltpu.CompilerParams(vmem_limit_bytes=32 * 1024 * 1024),
        name="attend",
    )(table, received, near, far)

    parts = lax.all_to_all(
        parts.reshape(16, PART + 8, HEAD), plane, split_axis=0, concat_axis=0, tiled=True
    )
    parts = pltpu.with_memory_space_constraint(parts.reshape(2, 8, PART + 8, HEAD), pltpu.VMEM)
    return pl.pallas_call(
        join_kernel,
        out_shape=jax.ShapeDtypeStruct(queries.shape, queries.dtype),
        in_specs=[vmem],
        out_specs=vmem,
        scratch_shapes=[pltpu.VMEM((8 * PART, HEAD), jnp.float32)],
        name="join",
    )(parts)


def solution(mesh):
    fine = Mesh(mesh.devices.reshape(2, Z, 2, 2, 4), ("yh", "z", "c", "yl", "x"))
    rows = P(("yh", "z", "c", "yl", "x"), None)
    return jax.shard_map(
        body,
        mesh=fine,
        in_specs=(rows, rows, rows, P(), P()),
        out_specs=rows,
        check_vma=False,
    )
```

```python
import math

import jax
import jax.numpy as jnp
from jax import lax
from jax.experimental import pallas as pl
from jax.experimental.pallas import tpu as pltpu
from jax.sharding import Mesh
from jax.sharding import PartitionSpec as P

GROUP = 8
HEAD = 128
BLK = 48
NB = 128
Z = 16
SLOTS = 64
CHUNK = 8 * BLK
ROWS = BLK * GROUP
PART = ROWS // 4
SCALE2 = math.log2(math.e) / math.sqrt(HEAD)
LOW = -1e30


def nn(a, b):
    return lax.dot_general(a, b, (((1,), (0,)), ((), ())), preferred_element_type=jnp.float32)


def nt(a, b):
    return lax.dot_general(a, b, (((1,), (1,)), ((), ())), preferred_element_type=jnp.float32)


def table_kernel(parent, slot, table):
    yh, z, c = lax.axis_index("yh"), lax.axis_index("z"), lax.axis_index("c")
    square = (NB, NB)
    row = lax.broadcasted_iota(jnp.int32, square, 0)
    column = lax.broadcasted_iota(jnp.int32, square, 1)
    one = lambda hit: jnp.where(hit, 1.0, 0.0).astype(jnp.bfloat16)
    reach_t = one((parent[...] == row) | (row == column))
    for _ in range(NB.bit_length() - 2):
        reach_t = one(nn(reach_t, reach_t) > 0.5)
    place = one(slot[...] == row)
    s = lax.broadcasted_iota(jnp.int32, (16, NB), 0)
    j = lax.broadcasted_iota(jnp.int32, (16, NB), 1)
    mine = (((s // 2) * Z + z) * 2 + c) * 2 + s % 2
    block = nt(one(j == mine), place).astype(jnp.bfloat16)
    reached = one(nt(one(nt(block, reach_t) > 0.5), reach_t) > 0.5)
    core = jnp.where(column < SLOTS // 2, c, 1 - c)
    theirs = ((yh * Z + (column % (SLOTS // 2)) // 2) * 2 + core) * 2 + column % 2
    order = one((row == theirs) & (column < SLOTS))
    held = nn(place, order).astype(jnp.bfloat16)
    own = (s // 2 == yh) & (j == z * 2 + s % 2)
    taken = (nn(reached, held) > 0.5) & ~own
    before = nn(one(taken), one(row < column))
    at = jnp.where(taken, before, -1.0)
    number = j.astype(jnp.float32).astype(jnp.bfloat16)
    lists = jnp.zeros((16, NB), jnp.float32)
    for q in range(4):
        hit = one(at[q : q + 1, :] == row.astype(jnp.float32))
        lists = jnp.where(s == q, nt(number, hit), lists)
    counts = jnp.sum(jnp.where(taken, 1.0, 0.0), axis=1, keepdims=True)
    last = (s // 2 == yh) & (j.astype(jnp.float32) == counts)
    lists = jnp.where(last, (z * 2 + s % 2).astype(jnp.float32), lists)
    lists = lists[:4].astype(jnp.int32)
    table[...] = jnp.concatenate([lists, jnp.broadcast_to(counts[:4], (4, NB)).astype(jnp.int32)], axis=0)


def pack_kernel(queries, keys, values, sent, spread):
    tokens = PART // GROUP
    for g in range(8):
        for h in range(GROUP):
            at = (g * GROUP + h) * HEAD
            rows = pl.ds(h, tokens, stride=GROUP)
            spread[g, rows, :] = queries[:, at : at + HEAD].astype(jnp.float32)
        columns = slice(g * HEAD, (g + 1) * HEAD)
        spread[g, PART : PART + tokens, :] = keys[:, columns].astype(jnp.float32)
        spread[g, PART + tokens :, :] = values[:, columns].astype(jnp.float32)
    for g in range(8):
        packed = spread[g].astype(jnp.bfloat16)
        sent[0, g] = packed
        sent[1, g] = packed


def unpack_kernel(received, pairs, spread):
    tokens = PART // GROUP
    for g in range(8):
        both = received[0, g, PART : PART + 2 * tokens, :].astype(jnp.float32)
        spread[g * tokens : (g + 1) * tokens, :HEAD] = both[:tokens]
        spread[g * tokens : (g + 1) * tokens, HEAD:] = both[tokens:]
    pairs[...] = spread[...].astype(jnp.bfloat16)


def attend_kernel(found, received, near, far, out, table, arrived, pairs, queries, scores, highest, totals, summed):
    yh = lax.axis_index("yh")
    half = SLOTS // 2 * BLK
    copy = pltpu.make_async_copy(found, table, arrived)
    copy.start()
    pairs[:half, :] = near[...]
    pairs[half:, :] = far[...]
    copy.wait()
    eye = lax.broadcasted_iota(jnp.int32, (PART, HEAD), 0) == lax.broadcasted_iota(
        jnp.int32, (PART, HEAD), 1
    )
    stat_row = lax.broadcasted_iota(jnp.int32, (16, HEAD), 0)
    tall = (ROWS, HEAD)
    tiles = CHUNK // HEAD
    least = lax.broadcasted_iota(jnp.int32, (1, CHUNK), 1)
    offset = lax.broadcasted_iota(jnp.int32, (ROWS, 1), 0) // GROUP
    last, bound = [], []
    for s in range(4):
        own = jnp.where(yh == s // 2, 1, 0)
        count = table[4 + s, 0]
        last.append(jnp.maximum(count + own - 1, 0) // 8)
        edge = (count - last[s] * 8) * BLK
        tail = jnp.where((least < edge + BLK) & (own > 0), least - edge, NB)
        bound.append(jnp.where(least < edge, 0, tail))

    def gathered(s, i, n, columns):
        places = [pl.multiple_of(table[s, i * 8 + t] * BLK, 16) for t in range(8 * n)]
        return jnp.concatenate([pairs[pl.ds(place, BLK), columns] for place in places], axis=0)

    def ready(s):
        for x in range(4):
            queries[s % 2][x * PART : (x + 1) * PART, :] = received[s // 2, s % 2 * 4 + x, :PART, :]
        highest[s % 2][...] = jnp.full(tall, LOW, jnp.float32)

    def score(s, i, n, masked):
        raw = nt(queries[s % 2][...], gathered(s, i, n, slice(0, HEAD)))
        top = highest[s % 2][...]
        for j in range(n):
            part = raw[:, j * CHUNK : (j + 1) * CHUNK]
            if masked and j == n - 1:
                part = jnp.where(offset >= bound[s], part, LOW)
            scores[s % 2][i + j] = part
            for k in range(tiles):
                top = jnp.maximum(top, part[:, k * HEAD : (k + 1) * HEAD])
        highest[s % 2][...] = top

    def weigh(s, i, n, masked):
        top = highest[s % 2][...]
        total = totals[...]
        weights = []
        for j in range(n):
            for k in range(tiles):
                columns = slice(k * HEAD, (k + 1) * HEAD)
                exponent = jnp.exp2((scores[s % 2][i + j, :, columns] - top) * SCALE2)
                if masked and j == n - 1:
                    exponent = jnp.where(offset >= bound[s][:, columns], exponent, 0.0)
                total = total + exponent
                weights.append(exponent.astype(jnp.bfloat16))
        totals[...] = total
        summed[...] += nn(jnp.concatenate(weights, axis=1), gathered(s, i, n, slice(HEAD, 2 * HEAD)))

    def run(*work):
        whole = [last[s] // 3 for _, s in work]
        together = whole[0] if len(work) == 1 else jnp.minimum(*whole)

        @pl.loop(0, together)
        def _(i):
            for step, s in work:
                step(s, 3 * i, 3, False)

        if len(work) > 1:
            for (step, s), end in zip(work, whole):

                @pl.loop(together, end)
                def _(i, step=step, s=s):
                    step(s, 3 * i, 3, False)

        for case in range(3 ** len(work)):
            extra = [case // 3**w % 3 for w in range(len(work))]
            here = [last[s] % 3 == extra[w] for w, (_, s) in enumerate(work)]

            @pl.when(here[0] if len(work) == 1 else here[0] & here[1])
            def _(extra=extra):
                for (step, s), more in zip(work, extra):
                    step(s, last[s] - more, 1 + more, True)

    ready(0)
    run((score, 0))
    for s in range(4):
        high = jnp.max(highest[s % 2][...], axis=1, keepdims=True)
        highest[s % 2][...] = jnp.broadcast_to(high, tall)
        totals[...] = jnp.zeros(tall, jnp.float32)
        summed[...] = jnp.zeros(tall, jnp.float32)
        if s < 3:
            ready(s + 1)
            run((weigh, s), (score, s + 1))
        else:
            run((weigh, s))
        total = jnp.sum(totals[...], axis=1, keepdims=True)
        some = total > 0.0
        safe = jnp.where(some, total, 1.0)
        result = (summed[...] * (1.0 / safe)).astype(jnp.bfloat16)
        size = jnp.where(some, high * SCALE2 + jnp.log2(safe), LOW)
        for x in range(4):
            rows = slice(x * PART, (x + 1) * PART)
            out[s, x, :PART, :] = result[rows, :]
            flat = jnp.sum(jnp.where(eye, size[rows, :], 0.0), axis=0, keepdims=True)
            first = flat.astype(jnp.bfloat16).astype(jnp.float32)
            second = (flat - first).astype(jnp.bfloat16).astype(jnp.float32)
            third = flat - first - second
            stats = jnp.where(
                stat_row == 0, first, jnp.where(stat_row == 1, second, jnp.where(stat_row == 2, third, 0.0))
            )
            out[s, x, PART:, :] = stats.astype(jnp.bfloat16)


def join_kernel(parts, out, joined):
    eye = lax.broadcasted_iota(jnp.int32, (PART, HEAD), 0) == lax.broadcasted_iota(
        jnp.int32, (PART, HEAD), 1
    )
    tokens = PART // GROUP
    for g in range(8):
        sizes = [
            jnp.sum(parts[y, g, PART:, :].astype(jnp.float32), axis=0, keepdims=True)
            for y in range(2)
        ]
        top = jnp.maximum(sizes[0], sizes[1])
        shares = [jnp.exp2(size - top) for size in sizes]
        first = shares[0] / (shares[0] + shares[1])
        first = jnp.sum(jnp.where(eye, first, 0.0), axis=1, keepdims=True)
        one, other = [parts[y, g, :PART, :].astype(jnp.float32) for y in range(2)]
        joined[g * PART : (g + 1) * PART, :] = other + (one - other) * first
    for g in range(8):
        for h in range(GROUP):
            at = (g * GROUP + h) * HEAD
            rows = pl.ds(g * PART + h, tokens, stride=GROUP)
            out[:, at : at + HEAD] = joined[rows, :].astype(jnp.bfloat16)


def body(queries, keys, values, parent_block, slot_block):
    tokens = queries.shape[0]
    vmem = pl.BlockSpec(memory_space=pltpu.VMEM)
    plane = ("yh", "yl", "x")
    wide = PART + 2 * tokens
    sent = pl.pallas_call(
        pack_kernel,
        out_shape=pltpu.VMEM((2, 8, wide, HEAD), jnp.bfloat16),
        in_specs=[vmem, vmem, vmem],
        out_specs=vmem,
        scratch_shapes=[pltpu.VMEM((8, wide, HEAD), jnp.float32)],
        name="pack",
    )(queries, keys, values).reshape(16, wide, HEAD)
    received = lax.all_to_all(sent, plane, split_axis=0, concat_axis=0, tiled=True)
    received = pltpu.with_memory_space_constraint(received.reshape(2, 8, wide, HEAD), pltpu.VMEM)
    pairs = pl.pallas_call(
        unpack_kernel,
        out_shape=pltpu.VMEM((8 * tokens, 2 * HEAD), jnp.bfloat16),
        grid=(1,),
        in_specs=[pl.BlockSpec((1, 8, wide, HEAD), lambda i: (lax.axis_index("yh"), 0, 0, 0))],
        out_specs=pl.BlockSpec((8 * tokens, 2 * HEAD), lambda i: (0, 0)),
        scratch_shapes=[pltpu.VMEM((8 * tokens, 2 * HEAD), jnp.float32)],
        name="unpack",
    )(received)
    near = lax.all_gather(pairs, "z", axis=0, tiled=True)
    far = lax.ppermute(near, "c", [(0, 1), (1, 0)])

    table = pl.pallas_call(
        table_kernel,
        out_shape=pltpu.VMEM((8, NB), jnp.int32),
        in_specs=[vmem, vmem],
        out_specs=vmem,
        name="table",
    )(parent_block.reshape(1, NB), slot_block.reshape(1, NB))

    parts = pl.pallas_call(
        attend_kernel,
        out_shape=pltpu.VMEM((4, 4, PART + 16, HEAD), jnp.bfloat16),
        in_specs=[pl.BlockSpec(memory_space=pl.ANY), vmem, vmem, vmem],
        out_specs=vmem,
        scratch_shapes=[
            pltpu.SMEM((8, NB), jnp.int32),
            pltpu.SemaphoreType.DMA,
            pltpu.VMEM((SLOTS * BLK, 2 * HEAD), jnp.bfloat16),
            [pltpu.VMEM((ROWS, HEAD), jnp.bfloat16)] * 2,
            [pltpu.VMEM((SLOTS // 8, ROWS, CHUNK), jnp.float32)] * 2,
            [pltpu.VMEM((ROWS, HEAD), jnp.float32)] * 2,
            pltpu.VMEM((ROWS, HEAD), jnp.float32),
            pltpu.VMEM((ROWS, HEAD), jnp.float32),
        ],
        compiler_params=pltpu.CompilerParams(vmem_limit_bytes=32 * 1024 * 1024),
        name="attend",
    )(table, received, near, far)

    parts = lax.all_to_all(
        parts.reshape(16, PART + 16, HEAD), plane, split_axis=0, concat_axis=0, tiled=True
    )
    parts = pltpu.with_memory_space_constraint(parts.reshape(2, 8, PART + 16, HEAD), pltpu.VMEM)
    return pl.pallas_call(
        join_kernel,
        out_shape=jax.ShapeDtypeStruct(queries.shape, queries.dtype),
        in_specs=[vmem],
        out_specs=vmem,
        scratch_shapes=[pltpu.VMEM((8 * PART, HEAD), jnp.float32)],
        name="join",
    )(parts)


def solution(mesh):
    fine = Mesh(mesh.devices.reshape(2, Z, 2, 2, 4), ("yh", "z", "c", "yl", "x"))
    rows = P(("yh", "z", "c", "yl", "x"), None)
    return jax.shard_map(
        body,
        mesh=fine,
        in_specs=(rows, rows, rows, P(), P()),
        out_specs=rows,
        check_vma=False,
    )
```
